256 devices in a mesh: seq: 32 (over y, z), head: 8 (over x, core).
Axes of the slice: x: 4, y: 4, z: 8, core: 2. Of those that a mesh axis runs over, the one named last changes fastest.
Arguments:
- queries: bfloat16 [32768, 4096], P('seq', 'head'), may hold values from -6 to 6
- keys: bfloat16 [32768, 4096], P('seq', 'head'), may hold values from -6 to 6
- values: bfloat16 [32768, 4096], P('seq', 'head'), may hold values from -6.6 to 6.6, as said below
- d_normed: bfloat16 [32768, 4096], P('seq', 'head'), may hold values from -6 to 6
- gain: float32 [4096], P('head'), may hold values from 0.1 to 1.9
Outputs:
- d_queries: bfloat16 [32768, 4096], P('seq', 'head')
- d_keys: bfloat16 [32768, 4096], P('seq', 'head')
- d_values: bfloat16 [32768, 4096], P('seq', 'head')
The draws below stay inside these ranges and needn't reach their ends.
Inputs may be any that keep to these rules, and one draw needn't show every extreme that they name: `values`: entries are bounded.
All inputs are finite; a program needn't handle non-finite values.
Results may differ from the reference program's by a relative error of at most 0.0058.
Values sent between devices are 32-bit elements; how exact they have to be, the bound alone decides.
A program may use at most 128 MiB of HBM per device.

```python
import jax
import jax.numpy as jnp
from jax import lax

HEADS = 32
HD = 128
TOK_DEV = 1024
TOKENS = 32768


def draw_values(key, part):
    key = jax.random.fold_in(key, 7)
    scale_key, entry_key = jax.random.split(key)
    position = jnp.arange(HEADS, dtype=jnp.float32) / max(HEADS - 1, 1)
    jitter = jax.random.uniform(scale_key, (HEADS,), jnp.float32, 0.9, 1.1)
    scales = 0.55 ** (1.0 - position) * jitter
    entries = jnp.clip(jax.random.normal(entry_key, (TOKENS, HEADS, HD), jnp.float32), -6.0, 6.0)
    return (entries * scales[None, :, None]).reshape(TOKENS, HEADS * HD).astype(jnp.bfloat16)


def levels(key, dims, cuts, least, top_value):
    def one(dim, parts):
        heights = jax.random.uniform(jax.random.fold_in(jax.random.fold_in(key, 6), dim), (parts,), jnp.float32, least / len(cuts), top_value / len(cuts))
        return jnp.repeat(jnp.exp(heights), dims[dim] // parts).reshape((-1,) + (1,) * (len(dims) - dim - 1))

    loudness = one(*cuts[0])
    for cut in cuts[1:]:
        loudness = loudness * one(*cut)
    return loudness


def normal_values(key, dims, deviation, reach, shards=(), kind=jnp.bfloat16):
    factor_of = levels(key, dims, shards, -0.22, 0.18) if shards else 1.0
    drawn = jax.random.normal(key, dims, jnp.float32) * deviation * factor_of
    return jnp.minimum(jnp.maximum(drawn, -reach), reach).astype(kind)


def setup_inputs(seed: int = 0) -> dict:
    arg_keys = jax.random.split(jax.random.key(seed), 6)
    queries = normal_values(arg_keys[0], (TOKENS, HEADS * HD), 1.0, 6.0, ((0, 32), (1, 8)))
    keys = normal_values(arg_keys[1], (TOKENS, HEADS * HD), 1.0, 6.0, ((0, 32), (1, 8)))
    values = draw_values(jax.random.fold_in(arg_keys[5], 71), 0)
    d_normed = normal_values(arg_keys[3], (TOKENS, HEADS * HD), 1.0, 6.0, ((0, 32), (1, 8)))
    gain = jnp.clip(1.0 + 0.18 * jax.random.normal(arg_keys[4], (HEADS * HD,), jnp.float32), 0.1, 1.9)
    return dict(queries=queries, keys=keys, values=values, d_normed=d_normed, gain=gain)


eps = 1e-06
highest_precision = lax.Precision.HIGHEST

def reference(queries, keys, values, d_normed, gain):
    seg_count = queries.shape[0] // TOK_DEV

    def by_segment(array):
        return array.reshape(seg_count, TOK_DEV, HEADS, HD)
    query4 = by_segment(queries)
    key4 = by_segment(keys)
    value4 = by_segment(values)
    upstream4 = by_segment(d_normed)
    gain2 = gain.reshape(HEADS, HD)
    causal = jnp.tril(jnp.ones((TOK_DEV, TOK_DEV), dtype=bool))
    features = HEADS * HD
    local_key_value = jnp.einsum('sthk,sthv->shkv', key4.astype(jnp.float32), value4.astype(jnp.float32), precision=highest_precision)
    zero_state = jnp.zeros((1, HEADS, HD, HD), jnp.float32)
    kv_before = jnp.concatenate([zero_state, jnp.cumsum(local_key_value, axis=0)[:-1]], axis=0)
    kv_low = kv_before.astype(jnp.bfloat16)

    def score_block(query_portion, key_seg):
        raw_scores = jnp.einsum('ihd,jhd->hij', query_portion.astype(jnp.float32), key_seg.astype(jnp.float32), precision=highest_precision)
        return jnp.where(causal[None], raw_scores, 0.0).astype(jnp.bfloat16)

    def forward_seg(items):
        query_portion, key_seg, value_seg, upstream_seg, state_lower = items
        score_matrix = score_block(query_portion, key_seg)
        attended_rows = jnp.einsum('bzg,gbr->zbr', score_matrix.astype(jnp.float32), value_seg.astype(jnp.float32), precision=highest_precision)
        attended_rows = attended_rows + jnp.einsum('mgu,gua->mga', query_portion.astype(jnp.float32), state_lower.astype(jnp.float32), precision=highest_precision)
        scaled = upstream_seg.astype(jnp.float32) * gain2[None]
        inv_rms = lax.rsqrt(lax.optimization_barrier(jnp.sum(attended_rows * attended_rows, axis=(1, 2))) / features + eps)
        cross_mean = lax.optimization_barrier(jnp.sum(scaled * attended_rows, axis=(1, 2))) / features
        d_attended = inv_rms[:, None, None] * scaled - attended_rows * (inv_rms ** 3 * cross_mean)[:, None, None]
        return d_attended.astype(jnp.bfloat16)
    d_att4 = lax.map(forward_seg, (query4, key4, value4, upstream4, kv_low))
    own_grad = jnp.einsum('sthk,sthv->shkv', query4.astype(jnp.float32), d_att4.astype(jnp.float32), precision=highest_precision)
    suffix = jnp.cumsum(own_grad[::-1], axis=0)[::-1]
    grad_after = jnp.concatenate([suffix[1:], zero_state], axis=0)
    grad_low = grad_after.astype(jnp.bfloat16)

    def backward_seg(items):
        query_portion, key_seg, value_seg, d_att_seg, state_lower, grad_state = items
        score_matrix = score_block(query_portion, key_seg).astype(jnp.float32)
        query_full = query_portion.astype(jnp.float32)
        key_full = key_seg.astype(jnp.float32)
        value_full = value_seg.astype(jnp.float32)
        attended_grad_full = d_att_seg.astype(jnp.float32)
        state_full = state_lower.astype(jnp.float32)
        gradient_full = grad_state.astype(jnp.float32)
        raw_grad = jnp.einsum('ihd,jhd->hij', attended_grad_full, value_full, precision=highest_precision)
        score_gradient = jnp.where(causal[None], raw_grad, 0.0).astype(jnp.bfloat16).astype(jnp.float32)
        query_gradient = jnp.einsum('bzg,gbr->zbr', score_gradient, key_full, precision=highest_precision) + jnp.einsum('uel,eml->uem', attended_grad_full, state_full, precision=highest_precision)
        key_gradient = jnp.einsum('oly,loz->yoz', score_gradient, query_full, precision=highest_precision) + jnp.einsum('fzc,zdc->fzd', value_full, gradient_full, precision=highest_precision)
        value_gradient = jnp.einsum('oly,loz->yoz', score_matrix, attended_grad_full, precision=highest_precision) + jnp.einsum('mwz,wzl->mwl', key_full, gradient_full, precision=highest_precision)
        return (query_gradient.astype(jnp.bfloat16), key_gradient.astype(jnp.bfloat16), value_gradient.astype(jnp.bfloat16))
    d_query4, d_key4, d_value4 = lax.map(backward_seg, (query4, key4, value4, d_att4, kv_low, grad_low))
    whole_shape = (seg_count * TOK_DEV, HEADS * HD)
    return (d_query4.reshape(whole_shape), d_key4.reshape(whole_shape), d_value4.reshape(whole_shape))
```

```python
import functools

import jax
import jax.numpy as jnp
from jax import lax
from jax.experimental import pallas as pl
from jax.experimental.pallas import tpu as pltpu
from jax.sharding import PartitionSpec as P

MESH = pl.DeviceIdType.MESH
HD = 128
BLK = 256
eps = 1e-06
f32 = jnp.float32
bf16 = jnp.bfloat16

NN = (((1,), (0,)), ((), ()))
NT = (((1,), (1,)), ((), ()))
TN = (((0,), (0,)), ((), ()))


def dot(a, b, dims=NN):
    return lax.dot_general(a, b, dims, preferred_element_type=f32)


def thirds(x):
    hi = x.astype(bf16)
    rest = x - hi.astype(f32)
    mid = rest.astype(bf16)
    low = (rest - mid.astype(f32)).astype(bf16)
    return hi, mid, low


def kernel(
    n_seq, n_head,
    q_hbm, k_hbm, v_hbm, dn_hbm, gain_ref,
    dq_hbm, dk_hbm, dv_hbm,
    q, k, v, dn, qt, st, att, da, own, up, pre, kvb, kvlow, own2, up2, pre2, gb, dk_part, dv_part,
    dq_o, dk_o, dv_o, stat, stat_in,
    in_sem, out_sem, up_s, up_r, down_s, down_r, up2_s, up2_r, down2_s, down2_r, stat_s, stat_r, loc_sem,
):
    toks, feat = q.shape
    heads = feat // HD
    nb = toks // BLK
    rows = own.shape[0] // n_seq
    seq = lax.axis_index("seq")
    head = lax.axis_index("head")

    loads = [
        pltpu.make_async_copy(src, dst, in_sem.at[i])
        for i, (src, dst) in enumerate(((k_hbm, k), (v_hbm, v), (q_hbm, q), (dn_hbm, dn)))
    ]
    for c in loads:
        c.start()

    barrier = pltpu.get_barrier_semaphore()

    def greet_seq(d, _):
        pl.semaphore_signal(barrier, inc=1, device_id={"seq": lax.rem(seq + d, n_seq)}, device_id_type=MESH)
        return 0

    def greet_head(d, _):
        pl.semaphore_signal(barrier, inc=1, device_id={"head": lax.rem(head + d, n_head)}, device_id_type=MESH)
        return 0

    lax.fori_loop(1, n_seq, greet_seq, 0)
    lax.fori_loop(1, n_head, greet_head, 0)

    def cols(h):
        return slice(h * HD, (h + 1) * HD)

    def scatter(src, dst, send, recv):
        def step(d, _):
            peer = lax.rem(seq + d, n_seq)
            pltpu.make_async_remote_copy(
                src_ref=src.at[pl.ds(pl.multiple_of(peer * rows, rows), rows)],
                dst_ref=dst.at[pl.ds(pl.multiple_of(seq * rows, rows), rows)],
                send_sem=send, recv_sem=recv, device_id={"seq": peer}, device_id_type=MESH,
            ).start()
            return 0

        lax.fori_loop(1, n_seq, step, 0)
        mine = pl.ds(pl.multiple_of(seq * rows, rows), rows)
        dst[mine, :] = src[mine, :]

    def wait_all(buf, sem):
        part = buf.at[pl.ds(0, (n_seq - 1) * rows)]
        pltpu.make_async_copy(part, part, sem).wait()

    def prefix(src, dst, order):
        acc = jnp.zeros((rows, HD), f32)
        for s in order:
            dst[s * rows : (s + 1) * rows, :] = acc
            acc = acc + src[s * rows : (s + 1) * rows, :]

    row = lax.broadcasted_iota(jnp.int32, (BLK, BLK), 0)
    col = lax.broadcasted_iota(jnp.int32, (BLK, BLK), 1)

    loads[0].wait()
    loads[1].wait()
    for h in range(heads):
        own[h * HD : (h + 1) * HD, :] = dot(k[:, cols(h)], v[:, cols(h)], TN)
    pl.semaphore_wait(barrier, n_seq - 1 + n_head - 1)
    scatter(own, up, up_s, up_r)

    loads[2].wait()
    loads[3].wait()

    def lower(a, b, i):
        a_i = a[i * BLK : (i + 1) * BLK]
        diag = jnp.where(row >= col, dot(a_i, b[i * BLK : (i + 1) * BLK], NT), 0.0).astype(bf16)
        left = dot(a_i, b[: i * BLK], NT).astype(bf16) if i else None
        return left, diag

    def upper(a, b, j):
        a_j = a[j * BLK : (j + 1) * BLK]
        diag = jnp.where(col >= row, dot(a_j, b[j * BLK : (j + 1) * BLK], NT), 0.0).astype(bf16)
        right = dot(a_j, b[(j + 1) * BLK :], NT).astype(bf16) if j < nb - 1 else None
        return diag, right

    for h in range(heads):
        qh, kh, vh = q[:, cols(h)], k[:, cols(h)], v[:, cols(h)]
        for i in range(nb):
            left, diag = lower(qh, kh, i)
            out = dot(diag, vh[i * BLK : (i + 1) * BLK])
            if i:
                out = out + dot(left, vh[: i * BLK])
            att[i * BLK : (i + 1) * BLK, cols(h)] = out

    wait_all(up, up_r)
    prefix(up, pre, range(n_seq))
    scatter(pre, kvb, down_s, down_r)

    for h in range(heads):
        qh, kh = q[:, cols(h)], k[:, cols(h)]
        qt[h * HD : (h + 1) * HD, :] = qh.T
        for j in range(nb):
            diag, right = upper(kh, qh, j)
            st[h, j * BLK : (j + 1) * BLK, j * BLK : (j + 1) * BLK] = diag
            if j < nb - 1:
                st[h, j * BLK : (j + 1) * BLK, (j + 1) * BLK :] = right

    wait_all(kvb, down_r)
    kvlow[...] = kvb[...].astype(bf16)

    sq = jnp.zeros((toks, HD), f32)
    cross = jnp.zeros((toks, HD), f32)
    for h in range(heads):
        a = att[:, cols(h)] + dot(q[:, cols(h)], kvlow[h * HD : (h + 1) * HD, :])
        att[:, cols(h)] = a
        sq = sq + a * a
        cross = cross + dn[:, cols(h)].astype(f32) * gain_ref[:, cols(h)] * a
    ones = jnp.ones((8, 3 * HD), bf16)
    sub = lax.broadcasted_iota(jnp.int32, (8, HD), 0)
    for n, x in enumerate((sq, cross)):
        sums = dot(ones, jnp.concatenate(thirds(x), axis=1), NT)
        tile = jnp.zeros((8, HD), f32)
        for r in range(toks // HD):
            tile = jnp.where(sub == r, sums[:, r * HD : (r + 1) * HD], tile)
        stat[n * 8 : n * 8 + 8, :] = tile

    def send_stat(d, _):
        peer = lax.rem(head + d, n_head)
        pltpu.make_async_remote_copy(
            src_ref=stat, dst_ref=stat_in.at[head],
            send_sem=stat_s, recv_sem=stat_r, device_id={"head": peer}, device_id_type=MESH,
        ).start()
        return 0

    lax.fori_loop(1, n_head, send_stat, 0)
    stat_in[head] = stat[...]
    got = stat_in.at[pl.ds(0, n_head - 1)]
    pltpu.make_async_copy(got, got, stat_r).wait()
    total = stat_in[0]
    for p in range(1, n_head):
        total = total + stat_in[p]
    features = feat * n_head
    inv = lax.rsqrt(total[:8] / features + eps)
    coef = inv * inv * inv * (total[8:] / features)

    def per_token(tile):
        spread = jnp.concatenate([jnp.where(sub == r, tile, 0.0) for r in range(toks // HD)], axis=1)
        parts = jnp.concatenate([p.astype(f32) for p in thirds(spread)], axis=0).astype(bf16)
        return dot(parts, jnp.ones((24, HD), bf16), TN)

    inv_col = per_token(inv)
    coef_col = per_token(coef)
    for h in range(heads):
        scaled = dn[:, cols(h)].astype(f32) * gain_ref[:, cols(h)]
        d = (inv_col * scaled - att[:, cols(h)] * coef_col).astype(bf16)
        da[:, cols(h)] = d
        own2[h * HD : (h + 1) * HD, :] = dot(qt[h * HD : (h + 1) * HD, :], d)
    scatter(own2, up2, up2_s, up2_r)

    for h in range(heads):
        qh, kh, vh, dh = q[:, cols(h)], k[:, cols(h)], v[:, cols(h)], da[:, cols(h)]
        for i in range(nb):
            sl = slice(i * BLK, (i + 1) * BLK)
            left, diag = lower(dh, vh, i)
            out = dot(dh[sl], kvlow[h * HD : (h + 1) * HD, :], NT) + dot(diag, kh[sl])
            if i:
                out = out + dot(left, kh[: i * BLK])
            dq_o[sl, cols(h)] = out.astype(bf16)
    dq_out = pltpu.make_async_copy(dq_o, dq_hbm, out_sem.at[0])
    dq_out.start()

    wait_all(up2, up2_r)
    prefix(up2, pre2, reversed(range(n_seq)))
    scatter(pre2, gb, down2_s, down2_r)

    for h in range(heads):
        qh, kh, vh, dh = q[:, cols(h)], k[:, cols(h)], v[:, cols(h)], da[:, cols(h)]
        for j in range(nb):
            sl = slice(j * BLK, (j + 1) * BLK)
            diag, right = upper(vh, dh, j)
            out = dot(diag, qh[sl])
            if j < nb - 1:
                out = out + dot(right, qh[(j + 1) * BLK :])
            dk_part[sl, cols(h)] = out
            dv_part[sl, cols(h)] = dot(st[h, sl, j * BLK :], dh[j * BLK :])

    wait_all(gb, down2_r)
    for h in range(heads):
        g = gb[h * HD : (h + 1) * HD, :].astype(bf16)
        dk_o[:, cols(h)] = (dk_part[:, cols(h)] + dot(v[:, cols(h)], g, NT)).astype(bf16)
        dv_o[:, cols(h)] = (dv_part[:, cols(h)] + dot(k[:, cols(h)], g)).astype(bf16)
    dk_out = pltpu.make_async_copy(dk_o, dk_hbm, out_sem.at[1])
    dv_out = pltpu.make_async_copy(dv_o, dv_hbm, out_sem.at[2])
    dk_out.start()
    dv_out.start()
    for buf, sem in ((own, up_s), (pre, down_s), (own2, up2_s), (pre2, down2_s)):
        wait_all(buf, sem)
    pltpu.make_async_copy(got, got, stat_s).wait()
    for c in (dq_out, dk_out, dv_out):
        c.wait()


def solution(mesh):
    n_seq, n_head = mesh.shape["seq"], mesh.shape["head"]

    def local(queries, keys, values, d_normed, gain):
        toks, feat = queries.shape
        heads = feat // HD
        state = pltpu.VMEM((heads * HD, HD), f32)
        wide = pltpu.VMEM((toks, feat), bf16)
        wide32 = pltpu.VMEM((toks, feat), f32)
        anywhere = pl.BlockSpec(memory_space=pl.ANY)
        out = jax.ShapeDtypeStruct((toks, feat), bf16)
        return pl.pallas_call(
            functools.partial(kernel, n_seq, n_head),
            out_shape=(out, out, out),
            in_specs=[anywhere] * 4 + [pl.BlockSpec(memory_space=pltpu.VMEM)],
            out_specs=(anywhere,) * 3,
            scratch_shapes=[
                wide, wide, wide, wide,
                pltpu.VMEM((feat, toks), bf16),
                pltpu.VMEM((heads, toks, toks), bf16),
                wide32, wide,
                state, state, state, state, pltpu.VMEM((heads * HD, HD), bf16),
                state, state, state, state,
                wide32, wide32,
                wide, wide, wide,
                pltpu.VMEM((16, HD), f32),
                pltpu.VMEM((n_head, 16, HD), f32),
                pltpu.SemaphoreType.DMA((4,)),
                pltpu.SemaphoreType.DMA((3,)),
            ] + [pltpu.SemaphoreType.DMA] * 11,
            compiler_params=pltpu.CompilerParams(
                collective_id=0, has_side_effects=True, vmem_limit_bytes=48 * 1024 * 1024
            ),
            name="scan_and_grads",
        )(queries, keys, values, d_normed, gain.reshape(1, feat))

    in_specs = (P("seq", "head"), P("seq", "head"), P("seq", "head"), P("seq", "head"), P("head"))
    out_specs = (P("seq", "head"), P("seq", "head"), P("seq", "head"))
    return jax.shard_map(local, mesh=mesh, in_specs=in_specs, out_specs=out_specs, check_vma=False)
```

```python
import functools

import jax
import jax.numpy as jnp
from jax import lax
from jax.experimental import pallas as pl
from jax.experimental.pallas import tpu as pltpu
from jax.sharding import PartitionSpec as P

MESH = pl.DeviceIdType.MESH
HD = 128
BLK = 256
NZ = 8
CHUNKS = 2
eps = 1e-06
f32 = jnp.float32
bf16 = jnp.bfloat16

NN = (((1,), (0,)), ((), ()))
NT = (((1,), (1,)), ((), ()))
TN = (((0,), (0,)), ((), ()))


def dot(a, b, dims=NN):
    return lax.dot_general(a, b, dims, preferred_element_type=f32)


def kernel(
    n_seq, n_head,
    q_hbm, k_hbm, v_hbm, dn_hbm, gain_ref,
    dq_o, dk_o, dv_o,
    q, k, v, dn, qt, st, att, scaled, da, own, up, pre, kvb, kvlow, own2, up2, pre2, gb, dk_part, dv_part,
    sq_part, cross_part, stat, stat_in,
    in_sem, up_s, up_r, down_s, down_r, up2_s, up2_r, down2_s, down2_r, stat_s, stat_r,
):
    toks, feat = q.shape
    heads = feat // HD
    nb = toks // BLK
    hc = heads // CHUNKS
    crows = hc * HD
    rows = crows // n_seq
    ny = n_seq // NZ
    seq = lax.axis_index("seq")
    head = lax.axis_index("head")
    my_y, my_z = seq // NZ, lax.rem(seq, NZ)

    loads = [
        pltpu.make_async_copy(src, dst, in_sem.at[i])
        for i, (src, dst) in enumerate(((k_hbm, k), (v_hbm, v), (q_hbm, q), (dn_hbm, dn)))
    ]
    loads[0].start()
    loads[1].start()

    along_y = [lax.rem(my_y + d, ny) * NZ for d in range(ny)]
    along_z = [lax.rem(my_z + d, NZ) for d in range(NZ)]
    offsets = sorted(
        ((y, z) for y in range(ny) for z in range(NZ) if y or z),
        key=lambda o: -min(o[0], ny - o[0]) - min(o[1], NZ - o[1]),
    )
    peers = [along_y[y] + along_z[z] for y, z in offsets]

    barrier = pltpu.get_barrier_semaphore()

    for peer in peers:
        pl.semaphore_signal(barrier, inc=1, device_id={"seq": peer}, device_id_type=MESH)
    head_peers = [lax.rem(head + d, n_head) for d in range(1, n_head)]
    for peer in head_peers:
        pl.semaphore_signal(barrier, inc=1, device_id={"head": peer}, device_id_type=MESH)

    def cols(h):
        return slice(h * HD, (h + 1) * HD)

    def scatter(c, src, dst, send, recv):
        def at(j):
            return pl.ds(pl.multiple_of(c * crows + j * rows, rows), rows)

        for peer in peers:
            pltpu.make_async_remote_copy(
                src_ref=src.at[at(peer)], dst_ref=dst.at[at(seq)],
                send_sem=send.at[c], recv_sem=recv.at[c], device_id={"seq": peer}, device_id_type=MESH,
            ).start()
        dst[at(seq), :] = src[at(seq), :]

    def wait_all(c, buf, sem):
        part = buf.at[pl.ds(c * crows, (n_seq - 1) * rows)]
        pltpu.make_async_copy(part, part, sem.at[c]).wait()

    def prefix(c, src, dst, order):
        acc = jnp.zeros((rows, HD), f32)
        for s in order:
            sl = slice(c * crows + s * rows, c * crows + (s + 1) * rows)
            dst[sl, :] = acc
            acc = acc + src[sl, :]

    def chunk_heads(c):
        return range(c * hc, (c + 1) * hc)

    row = lax.broadcasted_iota(jnp.int32, (BLK, BLK), 0)
    col = lax.broadcasted_iota(jnp.int32, (BLK, BLK), 1)

    def lower(a, b, i):
        a_i = a[i * BLK : (i + 1) * BLK]
        diag = jnp.where(row >= col, dot(a_i, b[i * BLK : (i + 1) * BLK], NT), 0.0).astype(bf16)
        left = dot(a_i, b[: i * BLK], NT).astype(bf16) if i else None
        return left, diag

    def upper(a, b, j):
        a_j = a[j * BLK : (j + 1) * BLK]
        diag = jnp.where(col >= row, dot(a_j, b[j * BLK : (j + 1) * BLK], NT), 0.0).astype(bf16)
        right = dot(a_j, b[(j + 1) * BLK :], NT).astype(bf16) if j < nb - 1 else None
        return diag, right

    loads[0].wait()
    loads[1].wait()
    loads[2].start()
    loads[3].start()
    for h in range(heads):
        own[h * HD : (h + 1) * HD, :] = dot(k[:, cols(h)], v[:, cols(h)], TN)
    pl.semaphore_wait(barrier, n_seq - 1 + n_head - 1)
    for c in range(CHUNKS):
        scatter(c, own, up, up_s, up_r)

    loads[2].wait()
    loads[3].wait()
    for h in range(heads):
        qh, kh, vh = q[:, cols(h)], k[:, cols(h)], v[:, cols(h)]
        for i in range(nb):
            left, diag = lower(qh, kh, i)
            out = dot(diag, vh[i * BLK : (i + 1) * BLK])
            if i:
                out = out + dot(left, vh[: i * BLK])
            att[i * BLK : (i + 1) * BLK, cols(h)] = out

    for c in range(CHUNKS):
        wait_all(c, up, up_r)
        prefix(c, up, pre, range(n_seq))
        scatter(c, pre, kvb, down_s, down_r)

    for h in range(heads):
        qh, kh = q[:, cols(h)], k[:, cols(h)]
        qt[h * HD : (h + 1) * HD, :] = qh.T
        scaled[:, cols(h)] = dn[:, cols(h)].astype(f32) * gain_ref[:, cols(h)]
        for j in range(nb):
            diag, right = upper(kh, qh, j)
            st[h, j * BLK : (j + 1) * BLK, j * BLK : (j + 1) * BLK] = diag
            if j < nb - 1:
                st[h, j * BLK : (j + 1) * BLK, (j + 1) * BLK :] = right

    tiles = toks // HD
    for c in range(CHUNKS):
        wait_all(c, kvb, down_r)
        sq = cross = 0.0
        for h in chunk_heads(c):
            kvlow[h * HD : (h + 1) * HD, :] = kvb[h * HD : (h + 1) * HD, :].astype(bf16)
            a = att[:, cols(h)] + dot(q[:, cols(h)], kvlow[h * HD : (h + 1) * HD, :])
            att[:, cols(h)] = a
            sq = sq + a * a
            cross = cross + scaled[:, cols(h)] * a
        if c:
            sq = sq + sq_part[...]
            cross = cross + cross_part[...]
        if c < CHUNKS - 1:
            sq_part[...] = sq
            cross_part[...] = cross
    stat[:tiles, :] = jnp.sum(sq.reshape(tiles, HD, HD), axis=-1)
    stat[tiles:, :] = jnp.sum(cross.reshape(tiles, HD, HD), axis=-1)
    for peer in head_peers:
        pltpu.make_async_remote_copy(
            src_ref=stat, dst_ref=stat_in.at[head],
            send_sem=stat_s, recv_sem=stat_r, device_id={"head": peer}, device_id_type=MESH,
        ).start()
    stat_in[head] = stat[...]
    got = stat_in.at[pl.ds(0, n_head - 1)]
    pltpu.make_async_copy(got, got, stat_r).wait()
    total = stat_in[0]
    for i in range(1, n_head):
        total = total + stat_in[i]
    features = feat * n_head
    inv = lax.rsqrt(total[:tiles] / features + eps)
    coef = inv * inv * inv * (total[tiles:] / features)

    def per_token(tile):
        return jnp.concatenate([jnp.broadcast_to(tile[r : r + 1, :], (HD, HD)).T for r in range(tiles)], axis=0)

    inv_col = per_token(inv)
    coef_col = per_token(coef)
    for c in range(CHUNKS):
        for h in chunk_heads(c):
            d = (inv_col * scaled[:, cols(h)] - att[:, cols(h)] * coef_col).astype(bf16)
            da[:, cols(h)] = d
            own2[h * HD : (h + 1) * HD, :] = dot(qt[h * HD : (h + 1) * HD, :], d)
        scatter(c, own2, up2, up2_s, up2_r)

    for h in range(heads):
        qh, kh, vh, dh = q[:, cols(h)], k[:, cols(h)], v[:, cols(h)], da[:, cols(h)]
        for i in range(nb):
            sl = slice(i * BLK, (i + 1) * BLK)
            left, diag = lower(dh, vh, i)
            out = dot(dh[sl], kvlow[h * HD : (h + 1) * HD, :], NT) + dot(diag, kh[sl])
            if i:
                out = out + dot(left, kh[: i * BLK])
            dq_o[sl, cols(h)] = out.astype(bf16)

    for c in range(CHUNKS):
        wait_all(c, up2, up2_r)
        prefix(c, up2, pre2, reversed(range(n_seq)))
        scatter(c, pre2, gb, down2_s, down2_r)

    for h in range(heads):
        qh, vh, dh = q[:, cols(h)], v[:, cols(h)], da[:, cols(h)]
        for j in range(nb):
            sl = slice(j * BLK, (j + 1) * BLK)
            diag, right = upper(vh, dh, j)
            out = dot(diag, qh[sl])
            if j < nb - 1:
                out = out + dot(right, qh[(j + 1) * BLK :])
            dk_part[sl, cols(h)] = out
            dv_part[sl, cols(h)] = dot(st[h, sl, j * BLK :], dh[j * BLK :])

    for c in range(CHUNKS):
        wait_all(c, gb, down2_r)
        for h in chunk_heads(c):
            g = gb[h * HD : (h + 1) * HD, :].astype(bf16)
            dk_o[:, cols(h)] = (dk_part[:, cols(h)] + dot(v[:, cols(h)], g, NT)).astype(bf16)
            dv_o[:, cols(h)] = (dv_part[:, cols(h)] + dot(k[:, cols(h)], g)).astype(bf16)
    for c in range(CHUNKS):
        for buf, sem in ((own, up_s), (pre, down_s), (own2, up2_s), (pre2, down2_s)):
            wait_all(c, buf, sem)
    pltpu.make_async_copy(got, got, stat_s).wait()


def write_out(a, b, c, x, y, z, sem):
    copies = [pltpu.make_async_copy(s, d, sem.at[i]) for i, (s, d) in enumerate(((a, x), (b, y), (c, z)))]
    for copy in copies:
        copy.start()
    for copy in copies:
        copy.wait()


def solution(mesh):
    n_seq, n_head = mesh.shape["seq"], mesh.shape["head"]

    def local(queries, keys, values, d_normed, gain):
        toks, feat = queries.shape
        heads = feat // HD
        state = pltpu.VMEM((heads * HD, HD), f32)
        wide = pltpu.VMEM((toks, feat), bf16)
        wide32 = pltpu.VMEM((toks, feat), f32)
        anywhere = pl.BlockSpec(memory_space=pl.ANY)
        vmem = pl.BlockSpec(memory_space=pltpu.VMEM)
        pairs = pltpu.SemaphoreType.DMA((2,))
        grads = pl.pallas_call(
            functools.partial(kernel, n_seq, n_head),
            out_shape=(pltpu.VMEM((toks, feat), bf16),) * 3,
            in_specs=[anywhere] * 4 + [vmem],
            out_specs=(vmem,) * 3,
            scratch_shapes=[
                wide, wide, wide, wide,
                pltpu.VMEM((feat, toks), bf16),
                pltpu.VMEM((heads, toks, toks), bf16),
                wide32, wide32, wide,
                state, state, state, state, pltpu.VMEM((heads * HD, HD), bf16),
                state, state, state, state,
                wide32, wide32,
                pltpu.VMEM((toks, HD), f32), pltpu.VMEM((toks, HD), f32),
                pltpu.VMEM((2 * toks // HD, HD), f32),
                pltpu.VMEM((n_head, 2 * toks // HD, HD), f32),
                pltpu.SemaphoreType.DMA((4,)),
            ] + [pairs] * 8 + [pltpu.SemaphoreType.DMA] * 2,
            compiler_params=pltpu.CompilerParams(
                collective_id=0, has_side_effects=True, vmem_limit_bytes=58 * 1024 * 1024
            ),
            name="scan_and_grads",
        )(queries, keys, values, d_normed, gain.reshape(1, feat))
        out = jax.ShapeDtypeStruct((toks, feat), bf16)
        return pl.pallas_call(
            write_out,
            out_shape=(out,) * 3,
            in_specs=[vmem] * 3,
            out_specs=(anywhere,) * 3,
            scratch_shapes=[pltpu.SemaphoreType.DMA((3,))],
            compiler_params=pltpu.CompilerParams(vmem_limit_bytes=4 * 1024 * 1024),
            name="write_out",
        )(*[pltpu.with_memory_space_constraint(x, pltpu.VMEM) for x in grads])

    in_specs = (P("seq", "head"), P("seq", "head"), P("seq", "head"), P("seq", "head"), P("head"))
    out_specs = (P("seq", "head"), P("seq", "head"), P("seq", "head"))
    return jax.shard_map(local, mesh=mesh, in_specs=in_specs, out_specs=out_specs, check_vma=False)
```

```python
import functools

import jax
import jax.numpy as jnp
from jax import lax
from jax.experimental import pallas as pl
from jax.experimental.pallas import tpu as pltpu
from jax.sharding import PartitionSpec as P

MESH = pl.DeviceIdType.MESH
HD = 128
BLK = 256
NZ = 8
CHUNKS = 2
eps = 1e-06
f32 = jnp.float32
bf16 = jnp.bfloat16

NN = (((1,), (0,)), ((), ()))
NT = (((1,), (1,)), ((), ()))
TN = (((0,), (0,)), ((), ()))


def dot(a, b, dims=NN):
    return lax.dot_general(a, b, dims, preferred_element_type=f32)


def kernel(
    n_seq, n_head,
    q_hbm, k_hbm, v_hbm, dn_hbm, gain_hbm,
    dq_o, dk_o, dv_o, k, v, dk_late, dv_late, g_late,
    q, dn, qt, st, att, scaled, da, own, up, pre, kvb, kvlow, own2, up2, pre2, gb, dk_early, dv_early,
    gain_ref, sq_part, cross_part, stat, stat_in,
    in_sem, up_s, up_r, down_s, down_r, up2_s, up2_r, down2_s, down2_r, stat_s, stat_r,
):
    toks, feat = q.shape
    heads = feat // HD
    nb = toks // BLK
    hc = heads // CHUNKS
    crows = hc * HD
    rows = crows // n_seq
    ny = n_seq // NZ
    seq = lax.axis_index("seq")
    head = lax.axis_index("head")
    my_y, my_z = seq // NZ, lax.rem(seq, NZ)

    loads = [
        pltpu.make_async_copy(src, dst, in_sem.at[i])
        for i, (src, dst) in enumerate(((k_hbm, k), (v_hbm, v), (q_hbm, q), (dn_hbm, dn), (gain_hbm, gain_ref)))
    ]
    other = head + 1 - 2 * lax.rem(head, 2)
    along_y = [lax.rem(my_y + d, ny) * NZ for d in range(ny)]
    along_z = [lax.rem(my_z + d, NZ) for d in range(NZ)]
    offsets = sorted(
        ((y, z) for y in range(ny) for z in range(NZ)),
        key=lambda o: -min(o[0], ny - o[0]) - min(o[1], NZ - o[1]),
    )
    peers = [along_y[y] + along_z[z] for y, z in offsets]

    barrier = pltpu.get_barrier_semaphore()

    for peer in peers:
        pl.semaphore_signal(barrier, inc=1, device_id={"seq": peer, "head": other}, device_id_type=MESH)
    head_peers = [lax.rem(head + d, n_head) for d in range(1, n_head)]
    for peer in head_peers:
        pl.semaphore_signal(barrier, inc=1, device_id={"head": peer}, device_id_type=MESH)

    loads[0].start()
    loads[1].start()

    def cols(h):
        return slice(h * HD, (h + 1) * HD)

    def scatter(c, src, dst, send, recv):
        def at(j):
            return pl.ds(pl.multiple_of(c * crows + j * rows, rows), rows)

        for peer in peers:
            pltpu.make_async_remote_copy(
                src_ref=src.at[at(peer)], dst_ref=dst.at[at(seq)],
                send_sem=send.at[c], recv_sem=recv.at[c], device_id={"seq": peer, "head": other}, device_id_type=MESH,
            ).start()

    def wait_all(c, buf, sem):
        part = buf.at[pl.ds(c * crows, crows)]
        pltpu.make_async_copy(part, part, sem.at[c]).wait()

    def prefix(c, src, dst, order):
        acc = jnp.zeros((rows, HD), f32)
        for s in order:
            sl = slice(c * crows + s * rows, c * crows + (s + 1) * rows)
            dst[sl, :] = acc
            acc = acc + src[sl, :]

    def chunk_heads(c):
        return range(c * hc, (c + 1) * hc)

    row = lax.broadcasted_iota(jnp.int32, (BLK, BLK), 0)
    col = lax.broadcasted_iota(jnp.int32, (BLK, BLK), 1)

    def lower(a, b, i):
        a_i = a[i * BLK : (i + 1) * BLK]
        diag = jnp.where(row >= col, dot(a_i, b[i * BLK : (i + 1) * BLK], NT), 0.0).astype(bf16)
        left = dot(a_i, b[: i * BLK], NT).astype(bf16) if i else None
        return left, diag

    def upper(a, b, j):
        a_j = a[j * BLK : (j + 1) * BLK]
        diag = jnp.where(col >= row, dot(a_j, b[j * BLK : (j + 1) * BLK], NT), 0.0).astype(bf16)
        right = dot(a_j, b[(j + 1) * BLK :], NT).astype(bf16) if j < nb - 1 else None
        return diag, right

    loads[0].wait()
    loads[1].wait()
    for c in loads[2:]:
        c.start()
    for h in range(heads):
        own[h * HD : (h + 1) * HD, :] = dot(k[:, cols(h)], v[:, cols(h)], TN)
    pl.semaphore_wait(barrier, n_seq + n_head - 1)
    for c in range(CHUNKS):
        scatter(c, own, up, up_s, up_r)

    for c in loads[2:]:
        c.wait()
    def attend_own(h):
        qh, kh, vh = q[:, cols(h)], k[:, cols(h)], v[:, cols(h)]
        for i in range(nb):
            left, diag = lower(qh, kh, i)
            out = dot(diag, vh[i * BLK : (i + 1) * BLK])
            if i:
                out = out + dot(left, vh[: i * BLK])
            att[i * BLK : (i + 1) * BLK, cols(h)] = out

    for h in range(heads - 1):
        attend_own(h)

    def upper_scores(h):
        qh, kh = q[:, cols(h)], k[:, cols(h)]
        qt[h * HD : (h + 1) * HD, :] = qh.T
        scaled[:, cols(h)] = dn[:, cols(h)].astype(f32) * gain_ref[:, cols(h)]
        for j in range(nb):
            diag, right = upper(kh, qh, j)
            st[h, j * BLK : (j + 1) * BLK, j * BLK : (j + 1) * BLK] = diag
            if j < nb - 1:
                st[h, j * BLK : (j + 1) * BLK, (j + 1) * BLK :] = right

    def owner_step(src, ready, mid, back, send, recv, order, work):
        for c in range(CHUNKS):
            wait_all(c, src, ready)
            prefix(c, src, mid, order)
            scatter(c, mid, back, send, recv)
            work[c]()

    owner_step(up, up_r, pre, kvb, down_s, down_r, range(n_seq), (
        lambda: attend_own(heads - 1),
        lambda: [upper_scores(h) for h in range(heads)],
    ))

    tiles = toks // HD
    for c in range(CHUNKS):
        wait_all(c, kvb, down_r)
        sq = cross = 0.0
        for h in chunk_heads(c):
            kvlow[h * HD : (h + 1) * HD, :] = kvb[h * HD : (h + 1) * HD, :].astype(bf16)
            a = att[:, cols(h)] + dot(q[:, cols(h)], kvlow[h * HD : (h + 1) * HD, :])
            att[:, cols(h)] = a
            sq = sq + a * a
            cross = cross + scaled[:, cols(h)] * a
        if c:
            sq = sq + sq_part[...]
            cross = cross + cross_part[...]
        if c < CHUNKS - 1:
            sq_part[...] = sq
            cross_part[...] = cross
    stat[:tiles, :] = jnp.sum(sq.reshape(tiles, HD, HD), axis=-1)
    stat[tiles:, :] = jnp.sum(cross.reshape(tiles, HD, HD), axis=-1)
    for peer in head_peers:
        pltpu.make_async_remote_copy(
            src_ref=stat, dst_ref=stat_in.at[head],
            send_sem=stat_s, recv_sem=stat_r, device_id={"head": peer}, device_id_type=MESH,
        ).start()
    stat_in[head] = stat[...]
    got = stat_in.at[pl.ds(0, n_head - 1)]
    pltpu.make_async_copy(got, got, stat_r).wait()
    total = stat_in[0]
    for i in range(1, n_head):
        total = total + stat_in[i]
    features = feat * n_head
    inv = lax.rsqrt(total[:tiles] / features + eps)
    coef = inv * inv * inv * (total[tiles:] / features)

    def per_token(tile):
        return jnp.concatenate([jnp.broadcast_to(tile[r : r + 1, :], (HD, HD)).T for r in range(tiles)], axis=0)

    inv_col = per_token(inv)
    coef_col = per_token(coef)
    for c in range(CHUNKS):
        for h in chunk_heads(c):
            d = (inv_col * scaled[:, cols(h)] - att[:, cols(h)] * coef_col).astype(bf16)
            da[:, cols(h)] = d
            own2[h * HD : (h + 1) * HD, :] = dot(qt[h * HD : (h + 1) * HD, :], d)
        scatter(c, own2, up2, up2_s, up2_r)

    for h in range(heads):
        qh, kh, vh, dh = q[:, cols(h)], k[:, cols(h)], v[:, cols(h)], da[:, cols(h)]
        for i in range(nb):
            sl = slice(i * BLK, (i + 1) * BLK)
            left, diag = lower(dh, vh, i)
            out = dot(dh[sl], kvlow[h * HD : (h + 1) * HD, :], NT) + dot(diag, kh[sl])
            if i:
                out = out + dot(left, kh[: i * BLK])
            dq_o[sl, cols(h)] = out.astype(bf16)

    def upper_grads(h):
        qh, vh, dh = q[:, cols(h)], v[:, cols(h)], da[:, cols(h)]
        for j in range(nb):
            sl = slice(j * BLK, (j + 1) * BLK)
            diag, right = upper(vh, dh, j)
            out = dot(diag, qh[sl])
            if j < nb - 1:
                out = out + dot(right, qh[(j + 1) * BLK :])
            dk_part, dv_part = ((dk_early, dv_early), (dk_late, dv_late))[h // hc]
            dk_part[sl, cols(h % hc)] = out
            dv_part[sl, cols(h % hc)] = dot(st[h, sl, j * BLK :], dh[j * BLK :])

    owner_step(up2, up2_r, pre2, gb, down2_s, down2_r, range(n_seq - 1, -1, -1), (
        lambda: upper_grads(0),
        lambda: [upper_grads(h) for h in range(1, heads)],
    ))

    wait_all(0, gb, down2_r)
    for h in range(hc):
        g = gb[h * HD : (h + 1) * HD, :].astype(bf16)
        dk_o[:, cols(h)] = (dk_early[:, cols(h)] + dot(v[:, cols(h)], g, NT)).astype(bf16)
        dv_o[:, cols(h)] = (dv_early[:, cols(h)] + dot(k[:, cols(h)], g)).astype(bf16)
    wait_all(1, gb, down2_r)
    g_late[...] = gb[crows:, :].astype(bf16)
    for c in range(CHUNKS):
        for buf, sem in ((own, up_s), (pre, down_s), (own2, up2_s), (pre2, down2_s)):
            wait_all(c, buf, sem)
    pltpu.make_async_copy(got, got, stat_s).wait()


def finish(dq, dk, dv, k, v, dk_late, dv_late, g_late, dq_hbm, dk_hbm, dv_hbm, dk_o, dv_o, early_sem, late_sem):
    width = dk_late.shape[1]
    early = pl.ds(0, dq.shape[1] - width)
    copies = [
        pltpu.make_async_copy(src, dst, early_sem.at[i])
        for i, (src, dst) in enumerate(
            ((dq, dq_hbm), (dk.at[:, early], dk_hbm.at[:, early]), (dv.at[:, early], dv_hbm.at[:, early]))
        )
    ]
    for copy in copies:
        copy.start()
    for j in range(width // HD):
        here = slice(j * HD, (j + 1) * HD)
        there = slice(dq.shape[1] - width + j * HD, dq.shape[1] - width + (j + 1) * HD)
        g = g_late[here, :]
        dk_o[:, here] = (dk_late[:, here] + dot(v[:, there], g, NT)).astype(bf16)
        dv_o[:, here] = (dv_late[:, here] + dot(k[:, there], g)).astype(bf16)
        for i, (src, dst) in enumerate(((dk_o, dk_hbm), (dv_o, dv_hbm))):
            copy = pltpu.make_async_copy(
                src.at[:, pl.ds(j * HD, HD)], dst.at[:, pl.ds(dq.shape[1] - width + j * HD, HD)], late_sem.at[i, j]
            )
            copy.start()
            copies.append(copy)
    for copy in copies:
        copy.wait()


def solution(mesh):
    n_seq, n_head = mesh.shape["seq"], mesh.shape["head"]

    def local(queries, keys, values, d_normed, gain):
        toks, feat = queries.shape
        heads = feat // HD
        state = pltpu.VMEM((heads * HD, HD), f32)
        wide = pltpu.VMEM((toks, feat), bf16)
        wide32 = pltpu.VMEM((toks, feat), f32)
        half32 = pltpu.VMEM((toks, feat // CHUNKS), f32)
        half16 = pltpu.VMEM((toks, feat // CHUNKS), bf16)
        anywhere = pl.BlockSpec(memory_space=pl.ANY)
        vmem = pl.BlockSpec(memory_space=pltpu.VMEM)
        pairs = pltpu.SemaphoreType.DMA((2,))
        grads = pl.pallas_call(
            functools.partial(kernel, n_seq, n_head),
            out_shape=(wide,) * 5 + (half32, half32, pltpu.VMEM((feat // CHUNKS, HD), bf16)),
            in_specs=[anywhere] * 5,
            out_specs=(vmem,) * 8,
            scratch_shapes=[
                wide, wide,
                pltpu.VMEM((feat, toks), bf16),
                pltpu.VMEM((heads, toks, toks), bf16),
                wide32, wide32, wide,
                state, state, state, state, pltpu.VMEM((heads * HD, HD), bf16),
                state, state, state, state,
                half32, half32,
                pltpu.VMEM((1, feat), f32),
                pltpu.VMEM((toks, HD), f32), pltpu.VMEM((toks, HD), f32),
                pltpu.VMEM((2 * toks // HD, HD), f32),
                pltpu.VMEM((n_head, 2 * toks // HD, HD), f32),
                pltpu.SemaphoreType.DMA((5,)),
            ] + [pairs] * 8 + [pltpu.SemaphoreType.DMA] * 2,
            compiler_params=pltpu.CompilerParams(
                collective_id=0, has_side_effects=True, vmem_limit_bytes=56 * 1024 * 1024
            ),
            name="scan_and_grads",
        )(queries, keys, values, d_normed, gain.reshape(1, feat))
        out = jax.ShapeDtypeStruct((toks, feat), bf16)
        return pl.pallas_call(
            finish,
            out_shape=(out,) * 3,
            in_specs=[vmem] * 8,
            out_specs=(anywhere,) * 3,
            scratch_shapes=[half16, half16, pltpu.SemaphoreType.DMA((3,)), pltpu.SemaphoreType.DMA((2, feat // CHUNKS // HD))],
            compiler_params=pltpu.CompilerParams(vmem_limit_bytes=6 * 1024 * 1024),
            name="finish",
        )(*[pltpu.with_memory_space_constraint(x, pltpu.VMEM) for x in grads])

    in_specs = (P("seq", "head"), P("seq", "head"), P("seq", "head"), P("seq", "head"), P("head"))
    out_specs = (P("seq", "head"), P("seq", "head"), P("seq", "head"))
    return jax.shard_map(local, mesh=mesh, in_specs=in_specs, out_specs=out_specs, check_vma=False)
```

```python
import functools

import jax
import jax.numpy as jnp
from jax import lax
from jax.experimental import pallas as pl
from jax.experimental.pallas import tpu as pltpu
from jax.sharding import PartitionSpec as P

MESH = pl.DeviceIdType.MESH
HD = 128
BLK = 512
NZ = 8
CHUNKS = 2
eps = 1e-06
f32 = jnp.float32
bf16 = jnp.bfloat16

NN = (((1,), (0,)), ((), ()))
NT = (((1,), (1,)), ((), ()))
TN = (((0,), (0,)), ((), ()))


def dot(a, b, dims=NN):
    return lax.dot_general(a, b, dims, preferred_element_type=f32)


def kernel(
    n_seq, n_head,
    q_hbm, k_hbm, v_hbm, dn_hbm, gain_hbm,
    dq_o, dk_o, dv_o, k, v, dk_late, dv_late, g_late,
    q, dn, qt, st, att, scaled, da, own, up, pre, kvb, kvlow, own2, up2, pre2, gb, dk_early, dv_early,
    gain_ref, sq_part, cross_part, stat, stat_in,
    in_sem, up_s, up_r, down_s, down_r, up2_s, up2_r, down2_s, down2_r, stat_s, stat_r,
):
    toks, feat = q.shape
    heads = feat // HD
    nb = toks // BLK
    hc = heads // CHUNKS
    crows = hc * HD
    rows = crows // n_seq
    ny = n_seq // NZ
    seq = lax.axis_index("seq")
    head = lax.axis_index("head")
    my_y, my_z = seq // NZ, lax.rem(seq, NZ)

    loads = [
        pltpu.make_async_copy(src, dst, in_sem.at[i])
        for i, (src, dst) in enumerate(((k_hbm, k), (v_hbm, v), (q_hbm, q), (dn_hbm, dn), (gain_hbm, gain_ref)))
    ]
    other = head + 1 - 2 * lax.rem(head, 2)
    along_y = [lax.rem(my_y + d, ny) * NZ for d in range(ny)]
    along_z = [lax.rem(my_z + d, NZ) for d in range(NZ)]
    offsets = sorted(
        ((y, z) for y in range(ny) for z in range(NZ)),
        key=lambda o: -min(o[0], ny - o[0]) - min(o[1], NZ - o[1]),
    )
    peers = [along_y[y] + along_z[z] for y, z in offsets]

    barrier = pltpu.get_barrier_semaphore()

    for peer in peers:
        pl.semaphore_signal(barrier, inc=1, device_id={"seq": peer, "head": other}, device_id_type=MESH)
    head_peers = [lax.rem(head + d, n_head) for d in range(1, n_head)]
    for peer in head_peers:
        pl.semaphore_signal(barrier, inc=1, device_id={"head": peer}, device_id_type=MESH)

    loads[0].start()
    loads[1].start()

    def cols(h):
        return slice(h * HD, (h + 1) * HD)

    def scatter(c, src, dst, send, recv):
        def at(j):
            return pl.ds(pl.multiple_of(c * crows + j * rows, rows), rows)

        for peer in peers:
            pltpu.make_async_remote_copy(
                src_ref=src.at[at(peer)], dst_ref=dst.at[at(seq)],
                send_sem=send.at[c], recv_sem=recv.at[c], device_id={"seq": peer, "head": other}, device_id_type=MESH,
            ).start()

    def wait_all(c, buf, sem):
        part = buf.at[pl.ds(c * crows, crows)]
        pltpu.make_async_copy(part, part, sem.at[c]).wait()

    def prefix(c, src, dst, order):
        acc = jnp.zeros((rows, HD), f32)
        for s in order:
            sl = slice(c * crows + s * rows, c * crows + (s + 1) * rows)
            dst[sl, :] = acc
            acc = acc + src[sl, :]

    def chunk_heads(c):
        return range(c * hc, (c + 1) * hc)

    row = lax.broadcasted_iota(jnp.int32, (BLK, BLK), 0)
    col = lax.broadcasted_iota(jnp.int32, (BLK, BLK), 1)

    def lower(a, b, i):
        a_i = a[i * BLK : (i + 1) * BLK]
        diag = jnp.where(row >= col, dot(a_i, b[i * BLK : (i + 1) * BLK], NT), 0.0).astype(bf16)
        left = dot(a_i, b[: i * BLK], NT).astype(bf16) if i else None
        return left, diag

    def upper(a, b, j):
        a_j = a[j * BLK : (j + 1) * BLK]
        diag = jnp.where(col >= row, dot(a_j, b[j * BLK : (j + 1) * BLK], NT), 0.0).astype(bf16)
        right = dot(a_j, b[(j + 1) * BLK :], NT).astype(bf16) if j < nb - 1 else None
        return diag, right

    loads[0].wait()
    loads[1].wait()
    for c in loads[2:]:
        c.start()
    for h in range(heads):
        own[h * HD : (h + 1) * HD, :] = dot(k[:, cols(h)], v[:, cols(h)], TN)
    pl.semaphore_wait(barrier, n_seq + n_head - 1)
    for c in range(CHUNKS):
        scatter(c, own, up, up_s, up_r)

    for c in loads[2:]:
        c.wait()
    def attend_own(h):
        qh, kh, vh = q[:, cols(h)], k[:, cols(h)], v[:, cols(h)]
        for i in range(nb):
            left, diag = lower(qh, kh, i)
            out = dot(diag, vh[i * BLK : (i + 1) * BLK])
            if i:
                out = out + dot(left, vh[: i * BLK])
            att[i * BLK : (i + 1) * BLK, cols(h)] = out

    for h in range(heads - 1):
        attend_own(h)

    def upper_scores(h):
        qh, kh = q[:, cols(h)], k[:, cols(h)]
        qt[h * HD : (h + 1) * HD, :] = qh.T
        scaled[:, cols(h)] = dn[:, cols(h)].astype(f32) * gain_ref[:, cols(h)]
        for j in range(nb):
            diag, right = upper(kh, qh, j)
            st[h, j * BLK : (j + 1) * BLK, j * BLK : (j + 1) * BLK] = diag
            if j < nb - 1:
                st[h, j * BLK : (j + 1) * BLK, (j + 1) * BLK :] = right

    def owner_step(src, ready, mid, back, send, recv, order, work):
        for c in range(CHUNKS):
            wait_all(c, src, ready)
            prefix(c, src, mid, order)
            scatter(c, mid, back, send, recv)
            work[c]()

    owner_step(up, up_r, pre, kvb, down_s, down_r, range(n_seq), (
        lambda: attend_own(heads - 1),
        lambda: [upper_scores(h) for h in range(heads)],
    ))

    tiles = toks // HD
    for c in range(CHUNKS):
        wait_all(c, kvb, down_r)
        sq = cross = 0.0
        for h in chunk_heads(c):
            kvlow[h * HD : (h + 1) * HD, :] = kvb[h * HD : (h + 1) * HD, :].astype(bf16)
            a = att[:, cols(h)] + dot(q[:, cols(h)], kvlow[h * HD : (h + 1) * HD, :])
            att[:, cols(h)] = a
            sq = sq + a * a
            cross = cross + scaled[:, cols(h)] * a
        if c:
            sq = sq + sq_part[...]
            cross = cross + cross_part[...]
        if c < CHUNKS - 1:
            sq_part[...] = sq
            cross_part[...] = cross
    stat[:tiles, :] = jnp.sum(sq.reshape(tiles, HD, HD), axis=-1)
    stat[tiles:, :] = jnp.sum(cross.reshape(tiles, HD, HD), axis=-1)
    for peer in head_peers:
        pltpu.make_async_remote_copy(
            src_ref=stat, dst_ref=stat_in.at[head],
            send_sem=stat_s, recv_sem=stat_r, device_id={"head": peer}, device_id_type=MESH,
        ).start()
    stat_in[head] = stat[...]
    got = stat_in.at[pl.ds(0, n_head - 1)]
    pltpu.make_async_copy(got, got, stat_r).wait()
    total = stat_in[0]
    for i in range(1, n_head):
        total = total + stat_in[i]
    features = feat * n_head
    inv = lax.rsqrt(total[:tiles] / features + eps)
    coef = inv * inv * inv * (total[tiles:] / features)

    def per_token(tile):
        return jnp.concatenate([jnp.broadcast_to(tile[r : r + 1, :], (HD, HD)).T for r in range(tiles)], axis=0)

    inv_col = per_token(inv)
    coef_col = per_token(coef)
    for c in range(CHUNKS):
        for h in chunk_heads(c):
            d = (inv_col * scaled[:, cols(h)] - att[:, cols(h)] * coef_col).astype(bf16)
            da[:, cols(h)] = d
            own2[h * HD : (h + 1) * HD, :] = dot(qt[h * HD : (h + 1) * HD, :], d)
        scatter(c, own2, up2, up2_s, up2_r)

    for h in range(heads):
        qh, kh, vh, dh = q[:, cols(h)], k[:, cols(h)], v[:, cols(h)], da[:, cols(h)]
        for i in range(nb):
            sl = slice(i * BLK, (i + 1) * BLK)
            left, diag = lower(dh, vh, i)
            out = dot(dh[sl], kvlow[h * HD : (h + 1) * HD, :], NT) + dot(diag, kh[sl])
            if i:
                out = out + dot(left, kh[: i * BLK])
            dq_o[sl, cols(h)] = out.astype(bf16)

    def upper_grads(h):
        qh, vh, dh = q[:, cols(h)], v[:, cols(h)], da[:, cols(h)]
        for j in range(nb):
            sl = slice(j * BLK, (j + 1) * BLK)
            diag, right = upper(vh, dh, j)
            out = dot(diag, qh[sl])
            if j < nb - 1:
                out = out + dot(right, qh[(j + 1) * BLK :])
            dk_part, dv_part = ((dk_early, dv_early), (dk_late, dv_late))[h // hc]
            dk_part[sl, cols(h % hc)] = out
            dv_part[sl, cols(h % hc)] = dot(st[h, sl, j * BLK :], dh[j * BLK :])

    owner_step(up2, up2_r, pre2, gb, down2_s, down2_r, range(n_seq - 1, -1, -1), (
        lambda: upper_grads(0),
        lambda: [upper_grads(h) for h in range(1, heads)],
    ))

    wait_all(0, gb, down2_r)
    for h in range(hc):
        g = gb[h * HD : (h + 1) * HD, :].astype(bf16)
        dk_o[:, cols(h)] = (dk_early[:, cols(h)] + dot(v[:, cols(h)], g, NT)).astype(bf16)
        dv_o[:, cols(h)] = (dv_early[:, cols(h)] + dot(k[:, cols(h)], g)).astype(bf16)
    wait_all(1, gb, down2_r)
    g_late[...] = gb[crows:, :].astype(bf16)
    for c in range(CHUNKS):
        for buf, sem in ((own, up_s), (pre, down_s), (own2, up2_s), (pre2, down2_s)):
            wait_all(c, buf, sem)
    pltpu.make_async_copy(got, got, stat_s).wait()


def finish(dq, dk, dv, k, v, dk_late, dv_late, g_late, dq_hbm, dk_hbm, dv_hbm, dk_o, dv_o, early_sem, late_sem):
    width = dk_late.shape[1]
    early = pl.ds(0, dq.shape[1] - width)
    copies = [
        pltpu.make_async_copy(src, dst, early_sem.at[i])
        for i, (src, dst) in enumerate(
            ((dq, dq_hbm), (dk.at[:, early], dk_hbm.at[:, early]), (dv.at[:, early], dv_hbm.at[:, early]))
        )
    ]
    for copy in copies:
        copy.start()
    for j in range(width // HD):
        here = slice(j * HD, (j + 1) * HD)
        there = slice(dq.shape[1] - width + j * HD, dq.shape[1] - width + (j + 1) * HD)
        g = g_late[here, :]
        dk_o[:, here] = (dk_late[:, here] + dot(v[:, there], g, NT)).astype(bf16)
        dv_o[:, here] = (dv_late[:, here] + dot(k[:, there], g)).astype(bf16)
        for i, (src, dst) in enumerate(((dk_o, dk_hbm), (dv_o, dv_hbm))):
            copy = pltpu.make_async_copy(
                src.at[:, pl.ds(j * HD, HD)], dst.at[:, pl.ds(dq.shape[1] - width + j * HD, HD)], late_sem.at[i, j]
            )
            copy.start()
            copies.append(copy)
    for copy in copies:
        copy.wait()


def solution(mesh):
    n_seq, n_head = mesh.shape["seq"], mesh.shape["head"]

    def local(queries, keys, values, d_normed, gain):
        toks, feat = queries.shape
        heads = feat // HD
        state = pltpu.VMEM((heads * HD, HD), f32)
        wide = pltpu.VMEM((toks, feat), bf16)
        wide32 = pltpu.VMEM((toks, feat), f32)
        half32 = pltpu.VMEM((toks, feat // CHUNKS), f32)
        half16 = pltpu.VMEM((toks, feat // CHUNKS), bf16)
        anywhere = pl.BlockSpec(memory_space=pl.ANY)
        vmem = pl.BlockSpec(memory_space=pltpu.VMEM)
        pairs = pltpu.SemaphoreType.DMA((2,))
        grads = pl.pallas_call(
            functools.partial(kernel, n_seq, n_head),
            out_shape=(wide,) * 5 + (half32, half32, pltpu.VMEM((feat // CHUNKS, HD), bf16)),
            in_specs=[anywhere] * 5,
            out_specs=(vmem,) * 8,
            scratch_shapes=[
                wide, wide,
                pltpu.VMEM((feat, toks), bf16),
                pltpu.VMEM((heads, toks, toks), bf16),
                wide32, wide32, wide,
                state, state, state, state, pltpu.VMEM((heads * HD, HD), bf16),
                state, state, state, state,
                half32, half32,
                pltpu.VMEM((1, feat), f32),
                pltpu.VMEM((toks, HD), f32), pltpu.VMEM((toks, HD), f32),
                pltpu.VMEM((2 * toks // HD, HD), f32),
                pltpu.VMEM((n_head, 2 * toks // HD, HD), f32),
                pltpu.SemaphoreType.DMA((5,)),
            ] + [pairs] * 8 + [pltpu.SemaphoreType.DMA] * 2,
            compiler_params=pltpu.CompilerParams(
                collective_id=0, has_side_effects=True, vmem_limit_bytes=56 * 1024 * 1024
            ),
            name="scan_and_grads",
        )(queries, keys, values, d_normed, gain.reshape(1, feat))
        out = jax.ShapeDtypeStruct((toks, feat), bf16)
        return pl.pallas_call(
            finish,
            out_shape=(out,) * 3,
            in_specs=[vmem] * 8,
            out_specs=(anywhere,) * 3,
            scratch_shapes=[half16, half16, pltpu.SemaphoreType.DMA((3,)), pltpu.SemaphoreType.DMA((2, feat // CHUNKS // HD))],
            compiler_params=pltpu.CompilerParams(vmem_limit_bytes=6 * 1024 * 1024),
            name="finish",
        )(*[pltpu.with_memory_space_constraint(x, pltpu.VMEM) for x in grads])

    in_specs = (P("seq", "head"), P("seq", "head"), P("seq", "head"), P("seq", "head"), P("head"))
    out_specs = (P("seq", "head"), P("seq", "head"), P("seq", "head"))
    return jax.shard_map(local, mesh=mesh, in_specs=in_specs, out_specs=out_specs, check_vma=False)
```
